32 devices in a mesh: gx: 4 (over x, core), gy: 8 (over z, y).
Axes of the slice: x: 2, y: 2, z: 4, core: 2. Of those that a mesh axis runs over, the one named last changes fastest.
Arguments:
- stem_first: float32 [4, 1024, 1024], P('gx', 'gy'), may hold values from -6 to 6
- cotangent: float32 [4, 1024, 1024], P('gx', 'gy'), may hold values from -6 to 6
- branch_first: float32 [1024, 1024], P(('gx', 'gy')), may hold values from -0.1875 to 0.1875
- branch_second: float32 [1024, 1024], P(('gx', 'gy')), may hold values from -0.1875 to 0.1875
- bond_first: int32 [1024], replicated, may hold values from 0 to 1023, each once
- bond_second: int32 [1024], replicated, may hold values from 0 to 1023, each once
Outputs:
- grad_stem: float32 [4, 1024, 1024], P('gx', 'gy')
- grad_first: float32 [1024, 1024], P(('gx', 'gy'))
- grad_second: float32 [1024, 1024], P(('gx', 'gy'))
The draws below stay inside these ranges and needn't reach their ends.
Inputs may be any that keep to these rules, and one draw needn't show every extreme that they name: `bond_first`: each a permutation of the numbers below 1024. `bond_second`: each a permutation of the numbers below 1024.
All inputs are finite; a program needn't handle non-finite values.
Results may differ from the reference program's by a relative error of at most 0.000098.
Values sent between devices are 32-bit elements; how exact they have to be, the bound alone decides.
No kernel may reach another device: no remote copies, remote signals or barrier semaphores. Data moves between devices by JAX's collectives and lax.ppermute only.
A program may use at most 64 MiB of HBM per device.

```python
import jax
import jax.numpy as jnp
from jax import lax

BOND = 1024
ROWS = 1024
N_GX = 4


def spiked(entries, rng, source, target, shards_of, factor):
    owner, partner = [(jnp.arange(entries.shape[axis_at]) // (entries.shape[axis_at] // shards_of)).reshape([-1 if axis == axis_at else 1 for axis in range(entries.ndim)]) for axis_at in (source, target)]
    chosen = jax.random.permutation(rng, shards_of)[partner]
    strong = (owner == chosen) | (owner == (partner + shards_of // 2) % shards_of)
    return jnp.where(strong, factor * entries, entries)


def levels(key, extent, pieces, least, largest):
    def one(dim, blocks):
        draws = jax.random.uniform(jax.random.fold_in(jax.random.fold_in(key, 6), dim), (blocks,), jnp.float32, least / len(pieces), largest / len(pieces))
        return jnp.repeat(jnp.exp(draws), extent[dim] // blocks).reshape((-1,) + (1,) * (len(extent) - dim - 1))

    level = one(*pieces[0])
    for cut in pieces[1:]:
        level = level * one(*cut)
    return level


def centred(stream_key, dims, scale, most, cuts=(), held_as=jnp.bfloat16):
    factor_of = levels(stream_key, dims, cuts, -0.22, 0.18) if cuts else 1.0
    values = jax.random.normal(stream_key, dims, jnp.float32) * scale * factor_of
    return jnp.minimum(jnp.maximum(values, -most), most).astype(held_as)


def gaussian_with(key, shape, spread, reach, cuts, heavy, kind=jnp.bfloat16):
    values = spread * jax.random.normal(key, shape, jnp.float32)
    if cuts:
        values = values * levels(key, shape, cuts, -0.22, 0.18)
    return jnp.clip(spiked(values, jax.random.fold_in(key, 3), *heavy), -reach, reach).astype(kind)


def setup_inputs(seed: int = 0) -> dict:
    key_list = jax.random.split(jax.random.key(seed), 7)
    stem_first = gaussian_with(key_list[0], (N_GX, ROWS, BOND), 1.0, 6.0, ((0, 4), (1, 8)), (1, 2, 8, 2.0), jnp.float32)
    cotangent = centred(key_list[1], (N_GX, ROWS, BOND), 1.0, 6.0, ((0, 4), (1, 8)), jnp.float32)
    branch_first = centred(key_list[2], (BOND, BOND), BOND ** -0.5, 0.1875, ((0, 32),), jnp.float32)
    branch_second = centred(key_list[3], (BOND, BOND), BOND ** -0.5, 0.1875, ((0, 32),), jnp.float32)
    bond_first = jax.random.permutation(key_list[4], BOND).astype(jnp.int32)
    bond_second = jax.random.permutation(key_list[5], BOND).astype(jnp.int32)
    return dict(stem_first=stem_first, cotangent=cotangent, branch_first=branch_first, branch_second=branch_second, bond_first=bond_first, bond_second=bond_second)


def inverse(ordering):
    return jnp.zeros_like(ordering).at[ordering].set(jnp.arange(ordering.shape[0], dtype=jnp.int32))

def product(left, right):
    return jnp.dot(left, right, precision=lax.Precision.HIGHEST, preferred_element_type=jnp.float32)

def regroup(field):
    groups, height, width = field.shape
    blocks = field.reshape(groups, height, groups, width // groups)
    return jnp.transpose(blocks, (2, 1, 0, 3)).reshape(groups, height, width)

def reference(stem_first, cotangent, branch_first, branch_second, bond_first, bond_second):
    groups, height, width = stem_first.shape
    factor = 1.0 / jnp.sqrt(jnp.float32(groups * height))
    placed_first = branch_first[inverse(bond_first)]
    placed_second = branch_second[inverse(bond_second)]
    stem_flat = stem_first.reshape(groups * height, width)
    cotan_flat = cotangent.reshape(groups * height, width)
    stem_mid = product(stem_flat, placed_first).reshape(groups, height, width)
    regrouped = regroup(stem_mid).reshape(groups * height, width)
    back_regrouped = product(cotan_flat, placed_second.T).reshape(groups, height, width)
    grad_second = product(regrouped[:, bond_second].T, cotan_flat) * factor
    back_mid = regroup(back_regrouped).reshape(groups * height, width)
    grad_first = product(stem_flat[:, bond_first].T, back_mid) * factor
    grad_stem = product(back_mid, placed_first.T).reshape(groups, height, width)
    return (grad_stem, grad_first, grad_second)
```

```python
import jax
import jax.numpy as jnp
from jax import lax
from jax.sharding import PartitionSpec as P


def product(left, right, contract):
    return lax.dot_general(
        left,
        right,
        (contract, ((), ())),
        precision=lax.Precision.HIGH,
        preferred_element_type=jnp.float32,
    )


def inverse(ordering):
    return jnp.zeros_like(ordering).at[ordering].set(jnp.arange(ordering.shape[0], dtype=jnp.int32))


def swap(block, mask):
    size = lax.axis_size("gx")
    return lax.ppermute(block, "gx", [(i, i ^ mask) for i in range(size)])


def masks(size):
    return [1 << bit for bit in range(size.bit_length() - 1)]


def gx_gather(block):
    held = {0: block}
    for mask in reversed(masks(lax.axis_size("gx"))):
        held.update({rel ^ mask: swap(held[rel], mask) for rel in list(held)})
    return [held[rel] for rel in range(len(held))]


def gx_reduce(blocks):
    held = dict(enumerate(blocks))
    for mask in masks(lax.axis_size("gx")):
        held = {rel: held[rel] + swap(held[rel ^ mask], mask) for rel in held if not rel & mask}
    return held[0]


def gx_exchange(blocks):
    return [block if rel == 0 else swap(block, rel) for rel, block in enumerate(blocks)]


def ring_order(size):
    return [i for i in range(size) if i % 2 == 0] + [i for i in reversed(range(size)) if i % 2]


def ring_step(block, step):
    order = ring_order(lax.axis_size("gy"))
    size = len(order)
    return lax.ppermute(block, "gy", [(order[k], order[(k + step) % size]) for k in range(size)])


def gy_gather(block):
    size = lax.axis_size("gy")
    half = block.shape[0] // 2
    pieces = [None] * size
    pieces[0] = block
    ahead = behind = block
    for step in range(1, size // 2):
        ahead, behind = ring_step(ahead, -1), ring_step(behind, 1)
        pieces[step], pieces[size - step] = ahead, behind
    pieces[size // 2] = jnp.concatenate([ring_step(ahead[:half], -1), ring_step(behind[half:], 1)], axis=0)
    return jnp.concatenate(pieces, axis=0)


def gy_reduce(blocks):
    size = lax.axis_size("gy")
    half = blocks[0].shape[0] // 2
    far = blocks[size // 2]
    ahead, behind = ring_step(far[:half], 1), ring_step(far[half:], -1)
    near, back = blocks[size // 2 - 1], blocks[size // 2 + 1]
    ahead = jnp.concatenate([near[:half] + ahead, near[half:]], axis=0)
    behind = jnp.concatenate([back[:half], back[half:] + behind], axis=0)
    for step in range(size // 2 - 2, 0, -1):
        ahead = blocks[step] + ring_step(ahead, 1)
        behind = blocks[size - step] + ring_step(behind, -1)
    return blocks[0] + ring_step(ahead, 1) + ring_step(behind, -1)


def on_device(stem_first, cotangent, branch_first, branch_second, bond_first, bond_second):
    groups, splits = lax.axis_size("gx"), lax.axis_size("gy")
    me_x, me_y = lax.axis_index("gx"), lax.axis_index("gy")
    height, width = stem_first.shape[1:]
    low = width // groups
    own = width // (groups * splits)
    factor = 1.0 / jnp.sqrt(jnp.float32(height * groups * splits))
    stem_rows = stem_first.reshape(height, width)
    cotan_rows = cotangent.reshape(height, width)

    partner = me_x ^ jnp.arange(groups, dtype=jnp.int32)
    order = jnp.array(ring_order(splits), jnp.int32)
    place = jnp.zeros_like(order).at[order].set(jnp.arange(splits, dtype=jnp.int32))
    ahead = order[(place[me_y] + jnp.arange(splits, dtype=jnp.int32)) % splits]
    rows = (
        partner[:, None, None] * low + ahead[None, :, None] * own + jnp.arange(own, dtype=jnp.int32)[None, None, :]
    ).reshape(width)
    bond_first, bond_second = bond_first[rows], bond_second[rows]
    bond_second = ((bond_second // low) ^ me_x) * low + bond_second % low
    back_first, back_second = inverse(bond_first), inverse(bond_second)

    block_first, block_second = gy_gather(branch_first), gy_gather(branch_second)
    cotan_all = jnp.concatenate(gx_gather(cotan_rows), axis=0)
    picked = jnp.take(stem_rows, bond_first, axis=1)
    picked = gx_exchange([picked[:, rel * low : (rel + 1) * low] for rel in range(groups)])
    picked = jnp.concatenate(picked, axis=0)

    mid = product(picked, block_first, ((1,), (0,)))
    mid = mid.reshape(groups, height, groups, low).transpose(2, 1, 0, 3).reshape(groups * height, width)
    mid = jnp.take(mid, bond_second, axis=1)
    regrouped = gx_reduce([mid[:, rel * low : (rel + 1) * low] for rel in range(groups)])
    regrouped = regrouped.reshape(groups, height, low)[partner].reshape(groups * height, low)
    outer_second = product(regrouped, cotan_all, ((0,), (0,)))
    grad_second = gy_reduce([outer_second[k * own : (k + 1) * own] for k in range(splits)])

    back = product(cotan_all, block_second, ((1,), (1,)))
    pieces = gx_gather(back)
    pieces = [
        jnp.concatenate([piece.reshape(groups, height, low)[h ^ rel] for h in range(groups)], axis=0)
        for rel, piece in enumerate(pieces)
    ]
    back_mid = jnp.take(jnp.concatenate(pieces, axis=1), back_second, axis=1)
    back_mid = back_mid.reshape(groups, height, groups, low).transpose(2, 1, 0, 3).reshape(groups * height, width)

    outer_first = product(picked, back_mid, ((0,), (0,)))
    grad_first = gy_reduce([outer_first[k * own : (k + 1) * own] for k in range(splits)])
    grad_first = grad_first.reshape(own, groups, low)[:, partner].reshape(own, width)

    turned = block_first.reshape(low, groups, low)[:, partner].reshape(low, width)
    grad = product(back_mid, turned, ((1,), (1,)))
    grad = gx_exchange([grad[rel * height : (rel + 1) * height] for rel in range(groups)])
    grad_stem = jnp.take(jnp.concatenate(grad, axis=1), back_first, axis=1).reshape(1, height, width)
    return (grad_stem, grad_first * factor, grad_second * factor)


def solution(mesh):
    return jax.shard_map(
        on_device,
        mesh=mesh,
        in_specs=(
            P("gx", "gy", None),
            P("gx", "gy", None),
            P(("gx", "gy"), None),
            P(("gx", "gy"), None),
            P(),
            P(),
        ),
        out_specs=(P("gx", "gy", None), P(("gx", "gy"), None), P(("gx", "gy"), None)),
        check_vma=False,
    )
```

```python
import functools

import jax
import jax.numpy as jnp
from jax import lax
from jax.experimental import pallas as pl
from jax.experimental.pallas import tpu as pltpu
from jax.sharding import PartitionSpec as P


def product(left, right, contract):
    return lax.dot_general(
        left,
        right,
        (contract, ((), ())),
        precision=lax.Precision.HIGH,
        preferred_element_type=jnp.float32,
    )


def inverse(ordering):
    return jnp.zeros_like(ordering).at[ordering].set(jnp.arange(ordering.shape[0], dtype=jnp.int32))


def swap(block, mask):
    size = lax.axis_size("gx")
    return lax.ppermute(block, "gx", [(i, i ^ mask) for i in range(size)])


def masks(size):
    return [1 << bit for bit in range(size.bit_length() - 1)]


def gx_gather(block):
    held = {0: block}
    for mask in reversed(masks(lax.axis_size("gx"))):
        held.update({rel ^ mask: swap(held[rel], mask) for rel in list(held)})
    return [held[rel] for rel in range(len(held))]


def gx_reduce(blocks):
    held = dict(enumerate(blocks))
    for mask in masks(lax.axis_size("gx")):
        held = {rel: held[rel] + swap(held[rel ^ mask], mask) for rel in held if not rel & mask}
    return held[0]


def gx_exchange(blocks):
    return [block if rel == 0 else swap(block, rel) for rel, block in enumerate(blocks)]


def ring_order(size):
    return [i for i in range(size) if i % 2 == 0] + [i for i in reversed(range(size)) if i % 2]


def ring_step(block, step):
    order = ring_order(lax.axis_size("gy"))
    size = len(order)
    return lax.ppermute(block, "gy", [(order[k], order[(k + step) % size]) for k in range(size)])


def gy_pieces(block):
    size = lax.axis_size("gy")
    half = block.shape[0] // 2
    pieces = [None] * size
    pieces[0] = block
    ahead = behind = block
    for step in range(1, size // 2):
        ahead, behind = ring_step(ahead, -1), ring_step(behind, 1)
        pieces[step], pieces[size - step] = ahead, behind
    pieces[size // 2 : size // 2 + 1] = [ring_step(ahead[:half], -1), ring_step(behind[half:], 1)]
    return pieces


def gy_gather(block):
    return jnp.concatenate(gy_pieces(block), axis=0)


def gy_reduce(blocks):
    size = lax.axis_size("gy")
    half = blocks[0].shape[0] // 2
    far = blocks[size // 2]
    ahead, behind = ring_step(far[:half], 1), ring_step(far[half:], -1)
    near, back = blocks[size // 2 - 1], blocks[size // 2 + 1]
    ahead = jnp.concatenate([near[:half] + ahead, near[half:]], axis=0)
    behind = jnp.concatenate([back[:half], back[half:] + behind], axis=0)
    for step in range(size // 2 - 2, 0, -1):
        ahead = blocks[step] + ring_step(ahead, 1)
        behind = blocks[size - step] + ring_step(behind, -1)
    return blocks[0] + ring_step(ahead, 1) + ring_step(behind, -1)


def plain(stem_first, cotangent, branch_first, branch_second, bond_first, bond_second):
    groups, splits = lax.axis_size("gx"), lax.axis_size("gy")
    me_x, me_y = lax.axis_index("gx"), lax.axis_index("gy")
    height, width = stem_first.shape[1:]
    low = width // groups
    own = width // (groups * splits)
    factor = 1.0 / jnp.sqrt(jnp.float32(height * groups * splits))
    stem_rows = stem_first.reshape(height, width)
    cotan_rows = cotangent.reshape(height, width)

    partner = me_x ^ jnp.arange(groups, dtype=jnp.int32)
    order = jnp.array(ring_order(splits), jnp.int32)
    place = jnp.zeros_like(order).at[order].set(jnp.arange(splits, dtype=jnp.int32))
    ahead = order[(place[me_y] + jnp.arange(splits, dtype=jnp.int32)) % splits]
    rows = (
        partner[:, None, None] * low + ahead[None, :, None] * own + jnp.arange(own, dtype=jnp.int32)[None, None, :]
    ).reshape(width)
    bond_first, bond_second = bond_first[rows], bond_second[rows]
    bond_second = ((bond_second // low) ^ me_x) * low + bond_second % low
    back_first, back_second = inverse(bond_first), inverse(bond_second)

    block_first, block_second = gy_gather(branch_first), gy_gather(branch_second)
    cotan_all = jnp.concatenate(gx_gather(cotan_rows), axis=0)
    picked = jnp.take(stem_rows, bond_first, axis=1)
    picked = gx_exchange([picked[:, rel * low : (rel + 1) * low] for rel in range(groups)])
    picked = jnp.concatenate(picked, axis=0)

    mid = product(picked, block_first, ((1,), (0,)))
    mid = mid.reshape(groups, height, groups, low).transpose(2, 1, 0, 3).reshape(groups * height, width)
    mid = jnp.take(mid, bond_second, axis=1)
    regrouped = gx_reduce([mid[:, rel * low : (rel + 1) * low] for rel in range(groups)])
    regrouped = regrouped.reshape(groups, height, low)[partner].reshape(groups * height, low)
    outer_second = product(regrouped, cotan_all, ((0,), (0,)))
    grad_second = gy_reduce([outer_second[k * own : (k + 1) * own] for k in range(splits)])

    back = product(cotan_all, block_second, ((1,), (1,)))
    pieces = gx_gather(back)
    pieces = [
        jnp.concatenate([piece.reshape(groups, height, low)[h ^ rel] for h in range(groups)], axis=0)
        for rel, piece in enumerate(pieces)
    ]
    back_mid = jnp.take(jnp.concatenate(pieces, axis=1), back_second, axis=1)
    back_mid = back_mid.reshape(groups, height, groups, low).transpose(2, 1, 0, 3).reshape(groups * height, width)

    outer_first = product(picked, back_mid, ((0,), (0,)))
    grad_first = gy_reduce([outer_first[k * own : (k + 1) * own] for k in range(splits)])
    grad_first = grad_first.reshape(own, groups, low)[:, partner].reshape(own, width)

    turned = block_first.reshape(low, groups, low)[:, partner].reshape(low, width)
    grad = product(back_mid, turned, ((1,), (1,)))
    grad = gx_exchange([grad[rel * height : (rel + 1) * height] for rel in range(groups)])
    grad_stem = jnp.take(jnp.concatenate(grad, axis=1), back_first, axis=1).reshape(1, height, width)
    return (grad_stem, grad_first * factor, grad_second * factor)


def split(value):
    high = value.astype(jnp.bfloat16)
    return high, (value - high.astype(jnp.float32)).astype(jnp.bfloat16)


def dot(left, right, contract):
    return lax.dot_general(left, right, (contract, ((), ())), preferred_element_type=jnp.float32)


def dot_parts(left, right, contract):
    return dot(left[0], right[0], contract) + dot(left[0], right[1], contract) + dot(left[1], right[0], contract)


def ring_owner(offset):
    size = lax.axis_size("gy")
    me = lax.axis_index("gy")
    place = jnp.where(me % 2 == 0, me // 2, size - 1 - me // 2)
    place = (place + offset) % size
    return jnp.where(place < size // 2, 2 * place, 2 * (size - 1 - place) + 1)


def group(rel):
    return lax.axis_index("gx") ^ rel


def piece_rows(own, size):
    found = []
    for k in range(size):
        found += [(k, 0, own)] if k != size // 2 else [(k, 0, own // 2), (k, own // 2, own // 2)]
    return found


def aligned(index, size):
    return pl.ds(pl.multiple_of(index * size, size), size)


def store_split(high_ref, low_ref, where, value):
    high_ref[where], low_ref[where] = split(value)


def load_branch(pieces, high_ref, low_ref, own):
    size = lax.axis_size("gy")
    for ref, (k, first, count) in zip(pieces, piece_rows(own, size), strict=True):
        start = pl.multiple_of(ring_owner(k) * own + first, count)
        store_split(high_ref, low_ref, pl.ds(start, count), ref[...])


def chosen(bond_ref, rel, low, width):
    columns = bond_ref[:, aligned(group(rel), low)]
    position = lax.broadcasted_iota(jnp.int32, (width, low), 0)
    return (position == columns).astype(jnp.bfloat16)


def pick_kernel(stem_ref, bond_ref, *out_refs):
    high, low_part = split(stem_ref[...])
    width = stem_ref.shape[1]
    for rel, out_ref in enumerate(out_refs):
        select = chosen(bond_ref, rel, out_ref.shape[1], width)
        out_ref[...] = dot(high, select, ((1,), (0,))) + dot(low_part, select, ((1,), (0,)))


def mid_kernel(groups, own, bond_ref, *refs):
    picked, refs = refs[:groups], refs[groups:]
    out_refs, (branch_high, branch_low), (mid_high, mid_low) = refs[-groups - 4 : -4], refs[-4:-2], refs[-2:]
    pieces = refs[: -groups - 4]
    height, low = picked[0].shape
    width = groups * low
    load_branch(pieces, branch_high, branch_low, own)
    branch = branch_high[...], branch_low[...]
    for rel, ref in enumerate(picked):
        high, low_part = split(dot_parts(split(ref[...]), branch, ((1,), (0,))))
        columns = aligned(group(rel), low)
        for h in range(groups):
            mid_high[h * height : (h + 1) * height, columns] = high[:, h * low : (h + 1) * low]
            mid_low[h * height : (h + 1) * height, columns] = low_part[:, h * low : (h + 1) * low]
    for rel, out_ref in enumerate(out_refs):
        select = chosen(bond_ref, rel, low, width)
        out_ref[...] = dot(mid_high[...], select, ((1,), (0,))) + dot(mid_low[...], select, ((1,), (0,)))


def back_kernel(groups, own, *refs):
    cotan, refs = refs[:groups], refs[groups:]
    pieces, (out_ref, cotan_high, cotan_low, branch_high, branch_low) = refs[:-5], refs[-5:]
    height = cotan[0].shape[0]
    load_branch(pieces, branch_high, branch_low, own)
    branch = branch_high[...], branch_low[...]
    for rel, ref in enumerate(cotan):
        parts = split(ref[...])
        rows = aligned(group(rel), height)
        cotan_high[rows], cotan_low[rows] = parts
        out_ref[rows] = dot_parts(parts, branch, ((1,), (1,)))


def put_blocks(total, out_refs, total_ref):
    own = out_refs[0].shape[0]
    total_ref[...] = total
    for k, out_ref in enumerate(out_refs):
        out_ref[...] = total_ref[aligned(ring_owner(k), own)]


def second_kernel(factor, near_ref, far_ref, cotan_high, cotan_low, *refs):
    out_refs, total_ref = refs[:-1], refs[-1]
    regrouped = (near_ref[...] + far_ref[...]) * factor
    parts = split(regrouped.T)
    put_blocks(dot_parts(parts, (cotan_high[...], cotan_low[...]), ((1,), (0,))), out_refs, total_ref)


def first_kernel(groups, factor, bond_ref, *refs):
    back, picked, refs = refs[:groups], refs[groups : 2 * groups], refs[2 * groups :]
    out_refs, (back_high, back_low, picked_high, picked_low, total_ref) = refs[:-5], refs[-5:]
    height, low = picked[0].shape
    width = groups * low
    total = None
    for rel, ref in enumerate(back):
        select = chosen(bond_ref, rel, low, width)
        high, low_part = split(ref[...])
        term = dot(high, select, ((1,), (1,))) + dot(low_part, select, ((1,), (1,)))
        total = term if total is None else total + term
    for h in range(groups):
        for a in range(groups):
            value = total[h * height : (h + 1) * height, a * low : (a + 1) * low]
            where = (slice(a * height, (a + 1) * height), slice(h * low, (h + 1) * low))
            store_split(back_high, back_low, where, value)
    for rel, ref in enumerate(picked):
        store_split(picked_high, picked_low, (slice(None), aligned(group(rel), height)), (ref[...] * factor).T)
    parts = (picked_high[...], picked_low[...])
    put_blocks(dot_parts(parts, (back_high[...], back_low[...]), ((1,), (0,))), out_refs, total_ref)


def stem_kernel(groups, back_high, back_low, branch_high, branch_low, *out_refs):
    height = out_refs[0].shape[0]
    branch = branch_high[...], branch_low[...]
    for rel, out_ref in enumerate(out_refs):
        rows = aligned(group(rel), height)
        out_ref[...] = dot_parts((back_high[rows], back_low[rows]), branch, ((1,), (1,)))


def place_kernel(bond_ref, *refs):
    blocks, out_ref = refs[:-1], refs[-1]
    total = None
    for rel, ref in enumerate(blocks):
        select = chosen(bond_ref, rel, ref.shape[1], out_ref.shape[1])
        high, low_part = split(ref[...])
        term = dot(high, select, ((1,), (1,))) + dot(low_part, select, ((1,), (1,)))
        total = term if total is None else total + term
    out_ref[...] = total


def call(kernel, name, outs, flops, scratch, *operands):
    moved = sum(x.size * x.dtype.itemsize for x in (*operands, *outs))
    whole = pl.BlockSpec(memory_space=pltpu.VMEM)
    return pl.pallas_call(
        kernel,
        name=name,
        out_shape=outs,
        in_specs=[whole] * len(operands),
        out_specs=[whole] * len(outs),
        scratch_shapes=scratch,
        compiler_params=pltpu.CompilerParams(vmem_limit_bytes=32 * 1024 * 1024),
        cost_estimate=pl.CostEstimate(flops=flops, bytes_accessed=moved, transcendentals=0),
    )(*operands)


def f32(*shape):
    return jax.ShapeDtypeStruct(shape, jnp.float32)


def b16(*shape):
    return jax.ShapeDtypeStruct(shape, jnp.bfloat16)


def on_device(stem_first, cotangent, branch_first, branch_second, bond_first, bond_second):
    groups, splits = lax.axis_size("gx"), lax.axis_size("gy")
    height, width = stem_first.shape[1:]
    low = width // groups
    own = width // (groups * splits)
    if groups != 4 or low % 128 or own % 32 or height % 128:
        return plain(stem_first, cotangent, branch_first, branch_second, bond_first, bond_second)
    factor = (height * groups * splits) ** -0.5
    tall = groups * height
    unit = 2 * height * width * width
    first_bond, second_bond = bond_first.reshape(1, width), bond_second.reshape(1, width)
    stem_rows, cotan_rows = stem_first.reshape(height, width), cotangent.reshape(height, width)
    blocks = [f32(own, width)] * splits

    picked = call(pick_kernel, "pick", [f32(height, low)] * groups, 2 * unit, [], stem_rows, first_bond)
    picked = gx_exchange(picked)
    pieces_first = gy_pieces(branch_first)
    cotan = gx_gather(cotan_rows)
    pieces_second = gy_pieces(branch_second)

    *partial, first_high, first_low = call(
        functools.partial(mid_kernel, groups, own),
        "mid",
        [f32(tall, low)] * groups + [b16(low, width)] * 2,
        3 * unit + 2 * groups * unit,
        [pltpu.VMEM((tall, width), jnp.bfloat16)] * 2,
        second_bond,
        *picked,
        *pieces_first,
    )
    back, cotan_high, cotan_low = call(
        functools.partial(back_kernel, groups, own),
        "back",
        [f32(tall, low)] + [b16(tall, width)] * 2,
        3 * unit,
        [pltpu.VMEM((low, width), jnp.bfloat16)] * 2,
        *cotan,
        *pieces_second,
    )
    near, far = partial[0] + swap(partial[1], 1), partial[2] + swap(partial[3], 1)
    outer_second = call(
        functools.partial(second_kernel, factor),
        "grad_second",
        blocks,
        3 * unit,
        [pltpu.VMEM((low, width), jnp.float32)],
        near,
        swap(far, 2),
        cotan_high,
        cotan_low,
    )
    grad_second = gy_reduce(outer_second)

    *outer_first, back_high, back_low = call(
        functools.partial(first_kernel, groups, factor),
        "grad_first",
        blocks + [b16(tall, width)] * 2,
        3 * unit + 2 * groups * unit,
        [pltpu.VMEM((low, tall), jnp.bfloat16)] * 2 + [pltpu.VMEM((low, width), jnp.float32)],
        second_bond,
        *gx_gather(back),
        *picked,
    )
    grad_first = gy_reduce(outer_first)
    grad = call(
        functools.partial(stem_kernel, groups),
        "grad_stem",
        [f32(height, low)] * groups,
        3 * unit,
        [],
        back_high,
        back_low,
        first_high,
        first_low,
    )
    grad = call(place_kernel, "place", [f32(height, width)], 2 * unit, [], first_bond, *gx_exchange(grad))[0]
    return grad.reshape(1, height, width), grad_first, grad_second


def solution(mesh):
    return jax.shard_map(
        on_device,
        mesh=mesh,
        in_specs=(
            P("gx", "gy", None),
            P("gx", "gy", None),
            P(("gx", "gy"), None),
            P(("gx", "gy"), None),
            P(),
            P(),
        ),
        out_specs=(P("gx", "gy", None), P(("gx", "gy"), None), P(("gx", "gy"), None)),
        check_vma=False,
    )
```

```python
import functools

import jax
import jax.numpy as jnp
from jax import lax
from jax.experimental import pallas as pl
from jax.experimental.pallas import tpu as pltpu
from jax.sharding import PartitionSpec as P


def product(left, right, contract):
    return lax.dot_general(
        left,
        right,
        (contract, ((), ())),
        precision=lax.Precision.HIGH,
        preferred_element_type=jnp.float32,
    )


def inverse(ordering):
    return jnp.zeros_like(ordering).at[ordering].set(jnp.arange(ordering.shape[0], dtype=jnp.int32))


def swap(block, mask):
    size = lax.axis_size("gx")
    return lax.ppermute(block, "gx", [(i, i ^ mask) for i in range(size)])


def masks(size):
    return [1 << bit for bit in range(size.bit_length() - 1)]


def gx_gather(block):
    held = {0: block}
    for mask in reversed(masks(lax.axis_size("gx"))):
        held.update({rel ^ mask: swap(held[rel], mask) for rel in list(held)})
    return [held[rel] for rel in range(len(held))]


def gx_reduce(blocks):
    held = dict(enumerate(blocks))
    for mask in masks(lax.axis_size("gx")):
        held = {rel: held[rel] + swap(held[rel ^ mask], mask) for rel in held if not rel & mask}
    return held[0]


def gx_exchange(blocks):
    return [block if rel == 0 else swap(block, rel) for rel, block in enumerate(blocks)]


def pair_exchange(near, away):
    away = swap(away, 2)
    return near, swap(near, 1), away, swap(away, 1)


def pair_blocks(refs):
    half = refs[0].shape[0] // 2
    return [ref[half:] if rel % 2 else ref[:half] for rel, ref in enumerate(refs)]


def ring_order(size):
    return [i for i in range(size) if i % 2 == 0] + [i for i in reversed(range(size)) if i % 2]


def ring_step(block, step):
    order = ring_order(lax.axis_size("gy"))
    size = len(order)
    return lax.ppermute(block, "gy", [(order[k], order[(k + step) % size]) for k in range(size)])


def ordered(value, *others):
    return lax.optimization_barrier((value, *others))[0]


class Ring:
    def __init__(self, block):
        self.size = lax.axis_size("gy")
        self.ahead = self.behind = block
        self.taken = 0
        self.last = []
        self.pieces = [block] + [None] * (self.size - 1)

    def after(self, *others):
        self.ahead, self.behind, *others = lax.optimization_barrier((self.ahead, self.behind, *others))
        return others

    def step(self):
        self.taken += 1
        if self.taken < self.size // 2:
            self.ahead, self.behind = ring_step(self.ahead, -1), ring_step(self.behind, 1)
            self.pieces[self.taken], self.pieces[self.size - self.taken] = self.ahead, self.behind
            self.last.append((self.ahead, self.behind))
            return
        half = self.ahead.shape[0] // 2
        halves = [ring_step(self.ahead[:half], -1), ring_step(self.behind[half:], 1)]
        self.pieces[self.taken : self.taken + 1] = halves


def gy_pieces(block):
    ring = Ring(block)
    for _ in range(ring.size // 2):
        ring.step()
    return ring.pieces


def gy_gather(block):
    return jnp.concatenate(gy_pieces(block), axis=0)


def gy_reduce(blocks, waits=()):
    size = lax.axis_size("gy")
    waits = dict(waits)
    half = blocks[0].shape[0] // 2
    far = blocks[size // 2]
    ahead, behind = ring_step(far[:half], 1), ring_step(far[half:], -1)
    near, back = blocks[size // 2 - 1], blocks[size // 2 + 1]
    ahead = jnp.concatenate([near[:half] + ahead, near[half:]], axis=0)
    behind = jnp.concatenate([back[:half], back[half:] + behind], axis=0)
    for step in range(size // 2 - 2, -1, -1):
        ahead, behind = lax.optimization_barrier((ahead, behind, *waits.get(size // 2 - 1 - step, ())))[:2]
        ahead, behind = ring_step(ahead, 1), ring_step(behind, -1)
        if step:
            ahead, behind = blocks[step] + ahead, blocks[size - step] + behind
    return blocks[0] + ahead + behind


def plain(stem_first, cotangent, branch_first, branch_second, bond_first, bond_second):
    groups, splits = lax.axis_size("gx"), lax.axis_size("gy")
    me_x, me_y = lax.axis_index("gx"), lax.axis_index("gy")
    height, width = stem_first.shape[1:]
    low = width // groups
    own = width // (groups * splits)
    factor = 1.0 / jnp.sqrt(jnp.float32(height * groups * splits))
    stem_rows = stem_first.reshape(height, width)
    cotan_rows = cotangent.reshape(height, width)

    partner = me_x ^ jnp.arange(groups, dtype=jnp.int32)
    order = jnp.array(ring_order(splits), jnp.int32)
    place = jnp.zeros_like(order).at[order].set(jnp.arange(splits, dtype=jnp.int32))
    ahead = order[(place[me_y] + jnp.arange(splits, dtype=jnp.int32)) % splits]
    rows = (
        partner[:, None, None] * low + ahead[None, :, None] * own + jnp.arange(own, dtype=jnp.int32)[None, None, :]
    ).reshape(width)
    bond_first, bond_second = bond_first[rows], bond_second[rows]
    bond_second = ((bond_second // low) ^ me_x) * low + bond_second % low
    back_first, back_second = inverse(bond_first), inverse(bond_second)

    block_first, block_second = gy_gather(branch_first), gy_gather(branch_second)
    cotan_all = jnp.concatenate(gx_gather(cotan_rows), axis=0)
    picked = jnp.take(stem_rows, bond_first, axis=1)
    picked = gx_exchange([picked[:, rel * low : (rel + 1) * low] for rel in range(groups)])
    picked = jnp.concatenate(picked, axis=0)

    mid = product(picked, block_first, ((1,), (0,)))
    mid = mid.reshape(groups, height, groups, low).transpose(2, 1, 0, 3).reshape(groups * height, width)
    mid = jnp.take(mid, bond_second, axis=1)
    regrouped = gx_reduce([mid[:, rel * low : (rel + 1) * low] for rel in range(groups)])
    regrouped = regrouped.reshape(groups, height, low)[partner].reshape(groups * height, low)
    outer_second = product(regrouped, cotan_all, ((0,), (0,)))
    grad_second = gy_reduce([outer_second[k * own : (k + 1) * own] for k in range(splits)])

    back = product(cotan_all, block_second, ((1,), (1,)))
    pieces = gx_gather(back)
    pieces = [
        jnp.concatenate([piece.reshape(groups, height, low)[h ^ rel] for h in range(groups)], axis=0)
        for rel, piece in enumerate(pieces)
    ]
    back_mid = jnp.take(jnp.concatenate(pieces, axis=1), back_second, axis=1)
    back_mid = back_mid.reshape(groups, height, groups, low).transpose(2, 1, 0, 3).reshape(groups * height, width)

    outer_first = product(picked, back_mid, ((0,), (0,)))
    grad_first = gy_reduce([outer_first[k * own : (k + 1) * own] for k in range(splits)])
    grad_first = grad_first.reshape(own, groups, low)[:, partner].reshape(own, width)

    turned = block_first.reshape(low, groups, low)[:, partner].reshape(low, width)
    grad = product(back_mid, turned, ((1,), (1,)))
    grad = gx_exchange([grad[rel * height : (rel + 1) * height] for rel in range(groups)])
    grad_stem = jnp.take(jnp.concatenate(grad, axis=1), back_first, axis=1).reshape(1, height, width)
    return (grad_stem, grad_first * factor, grad_second * factor)


def split(value):
    high = value.astype(jnp.bfloat16)
    return high, (value - high.astype(jnp.float32)).astype(jnp.bfloat16)


def dot(left, right, contract):
    return lax.dot_general(left, right, (contract, ((), ())), preferred_element_type=jnp.float32)


def dot_parts(left, right, contract):
    return dot(left[0], right[0], contract) + dot(left[0], right[1], contract) + dot(left[1], right[0], contract)


def ring_owner(offset):
    size = lax.axis_size("gy")
    me = lax.axis_index("gy")
    place = jnp.where(me % 2 == 0, me // 2, size - 1 - me // 2)
    place = (place + offset) % size
    return jnp.where(place < size // 2, 2 * place, 2 * (size - 1 - place) + 1)


def group(rel):
    return lax.axis_index("gx") ^ rel


def early_offsets(size):
    near = [k for k in range(size) if min(k, size - k) <= size // 4]
    return near, [k for k in range(size) if k not in near]


def aligned(index, size):
    return pl.ds(pl.multiple_of(index * size, size), size)


def store_split(high_ref, low_ref, where, value):
    high_ref[where], low_ref[where] = split(value)


def branch_rows(ref, own, part):
    return ref[...] if ref.shape[0] == own else ref[part * own : (part + 1) * own]


def chosen(bond_ref, rel, low, width):
    columns = bond_ref[:, aligned(group(rel), low)]
    position = lax.broadcasted_iota(jnp.int32, (width, low), 0)
    return (position == columns).astype(jnp.bfloat16)


def put_pairs(blocks, pair_refs):
    size = pair_refs[0].shape[0] // 2
    for rel, block in enumerate(blocks):
        pair_refs[rel // 2][rel % 2 * size : (rel % 2 + 1) * size] = block


def pack_kernel(first_ref, second_ref, pair_ref, done):
    own = first_ref.shape[0]
    copies = [
        pltpu.make_async_copy(ref, pair_ref.at[pl.ds(part * own, own)], done.at[part])
        for part, ref in enumerate((first_ref, second_ref))
    ]
    for copy in copies:
        copy.start()
    for copy in copies:
        copy.wait()


def pick_kernel(groups, stem_ref, bond_ref, *out_refs):
    high, low_part = split(stem_ref[...])
    width = stem_ref.shape[1]
    selects = [chosen(bond_ref, rel, width // groups, width) for rel in range(groups)]
    put_pairs([dot(high, one, ((1,), (0,))) + dot(low_part, one, ((1,), (0,))) for one in selects], out_refs)


def absorb(picked, branch, mid, groups):
    height, low = picked[0].shape[0] // 2, picked[0].shape[1]
    for rel, block in enumerate(pair_blocks(picked)):
        parts = split(block)
        columns = aligned(group(rel), low)
        for h in range(groups):
            cut = slice(h * low, (h + 1) * low)
            value = dot_parts(parts, (branch[0][:, cut], branch[1][:, cut]), ((1,), (0,)))
            store_split(*mid, (slice(h * height, (h + 1) * height), columns), value)


def put_picks(bond_ref, mid, out_refs):
    width = mid[0].shape[1]
    rows, low = mid[0].shape[0], out_refs[0].shape[1]
    for rel in range(width // low):
        select = chosen(bond_ref, rel, low, width)
        block = dot(mid[0][...], select, ((1,), (0,))) + dot(mid[1][...], select, ((1,), (0,)))
        out_refs[rel % 2][rel // 2 * rows : (rel // 2 + 1) * rows] = block


def mid_kernel(groups, bond_ref, *refs):
    picked, refs = refs[:groups], refs[groups:]
    out_refs, branch, mid = refs[-6:-4], refs[-4:-2], refs[-2:]
    own = branch[0].shape[0] // lax.axis_size("gy")
    for k, ref in enumerate(refs[:-6]):
        store_split(*branch, aligned(ring_owner(k), own), branch_rows(ref, own, 0))
    absorb(picked, branch, mid, groups)
    put_picks(bond_ref, mid, out_refs)


def gather_rows(pieces, rows, own):
    for k, ref in enumerate(pieces):
        store_split(*rows, slice(k * own, (k + 1) * own), branch_rows(ref, own, 1))


def early_back_kernel(groups, own, *refs):
    cotan, refs = refs[:groups], refs[groups:]
    pieces, (out_ref, cotan_high, cotan_low, *rows) = refs[:-5], refs[-5:]
    height = cotan[0].shape[0]
    gather_rows(pieces, rows, own)
    for rel, ref in enumerate(cotan):
        store_split(cotan_high, cotan_low, aligned(group(rel), height), ref[...])
    out_ref[...] = dot_parts((rows[0][...], rows[1][...]), (cotan_high[...], cotan_low[...]), ((1,), (1,)))


def late_back_kernel(own, cotan_high, cotan_low, *refs):
    pieces, (out_ref, *rows) = refs[:-3], refs[-3:]
    gather_rows(pieces, rows, own)
    out_ref[...] = dot_parts((rows[0][...], rows[1][...]), (cotan_high[...], cotan_low[...]), ((1,), (1,)))


def put_blocks(total, out_refs, total_ref):
    own = out_refs[0].shape[0]
    total_ref[...] = total
    for k, out_ref in enumerate(out_refs):
        out_ref[...] = total_ref[aligned(ring_owner(k), own)]


def second_kernel(factor, near_ref, far_ref, cotan_high, cotan_low, *refs):
    firsts, refs = refs[: (len(refs) - 1) // 2], refs[(len(refs) - 1) // 2 :]
    out_refs, total_ref = refs[:-1], refs[-1]
    own = firsts[0].shape[0]
    parts = split(((near_ref[...] + far_ref[...]) * factor).T)
    total_ref[...] = dot_parts(parts, (cotan_high[...], cotan_low[...]), ((1,), (0,)))
    for k, (ref, out_ref) in enumerate(zip(firsts, out_refs, strict=True)):
        out_ref[:own] = ref[...]
        out_ref[own:] = total_ref[aligned(ring_owner(k), own)]


def first_kernel(groups, factor, bond_ref, *refs):
    near, far, picked, refs = refs[:groups], refs[groups : 2 * groups], refs[2 * groups : 3 * groups], refs[3 * groups :]
    out_refs, (turned_high, turned_low, rows_high, rows_low, picked_high, picked_low, total_ref) = refs[:-7], refs[-7:]
    height, low = picked[0].shape[0] // 2, picked[0].shape[1]
    width = groups * low
    size = lax.axis_size("gy")
    own = low // size
    for pieces, offsets in zip((near, far), early_offsets(size)):
        for rel, ref in enumerate(pieces):
            for number, k in enumerate(offsets):
                where = aligned(group(rel) * size + ring_owner(k), own)
                store_split(rows_high, rows_low, where, ref[number * own : (number + 1) * own])
    position = lax.broadcasted_iota(jnp.int32, (width, width), 0)
    select = (position == bond_ref[...]).astype(jnp.bfloat16)
    total = dot(select, rows_high[...], ((1,), (0,))) + dot(select, rows_low[...], ((1,), (0,)))
    for h in range(groups):
        for a in range(groups):
            value = total[a * low : (a + 1) * low, h * height : (h + 1) * height]
            where = (slice(h * low, (h + 1) * low), slice(a * height, (a + 1) * height))
            store_split(turned_high, turned_low, where, value)
    for rel, block in enumerate(pair_blocks(picked)):
        store_split(picked_high, picked_low, (slice(None), aligned(group(rel), height)), (block * factor).T)
    parts = picked_high[...], picked_low[...]
    put_blocks(dot_parts(parts, (turned_high[...], turned_low[...]), ((1,), (1,))), out_refs, total_ref)


def stem_kernel(groups, branch_high, branch_low, turned_high, turned_low, *refs):
    out_refs, total_ref = refs[:-1], refs[-1]
    height = total_ref.shape[1] // groups
    branch, turned = (branch_high[...], branch_low[...]), (turned_high[...], turned_low[...])
    total_ref[...] = dot_parts(branch, turned, ((1,), (0,)))
    put_pairs([total_ref[:, aligned(group(rel), height)] for rel in range(groups)], out_refs)


def place_kernel(bond_ref, *refs):
    blocks, out_ref = refs[:-1], refs[-1]
    total = None
    for rel, block in enumerate(pair_blocks(blocks)):
        select = chosen(bond_ref, rel, block.shape[0], out_ref.shape[1])
        high, low_part = split(block.T)
        term = dot(high, select, ((1,), (1,))) + dot(low_part, select, ((1,), (1,)))
        total = term if total is None else total + term
    out_ref[...] = total


def call(kernel, name, outs, flops, scratch, *operands):
    moved = sum(x.size * x.dtype.itemsize for x in (*operands, *outs))
    whole = pl.BlockSpec(memory_space=pltpu.VMEM)
    return pl.pallas_call(
        kernel,
        name=name,
        out_shape=outs,
        in_specs=[whole] * len(operands),
        out_specs=[whole] * len(outs),
        scratch_shapes=scratch,
        compiler_params=pltpu.CompilerParams(vmem_limit_bytes=32 * 1024 * 1024),
        cost_estimate=pl.CostEstimate(flops=flops, bytes_accessed=moved, transcendentals=0),
    )(*operands)


def f32(*shape):
    return jax.ShapeDtypeStruct(shape, jnp.float32)


def b16(*shape):
    return jax.ShapeDtypeStruct(shape, jnp.bfloat16)


def on_device(stem_first, cotangent, branch_first, branch_second, bond_first, bond_second):
    groups, splits = lax.axis_size("gx"), lax.axis_size("gy")
    height, width = stem_first.shape[1:]
    low = width // groups
    own = width // (groups * splits)
    if groups != 4 or splits % 2 or splits < 8 or low % 128 or own % 32 or height % 128:
        return plain(stem_first, cotangent, branch_first, branch_second, bond_first, bond_second)
    factor = (height * groups * splits) ** -0.5
    tall = groups * height
    unit = 2 * height * width * width
    first_bond, second_bond = bond_first.reshape(1, width), bond_second.reshape(1, width)
    stem_rows, cotan_rows = stem_first.reshape(height, width), cotangent.reshape(height, width)
    blocks = [f32(own, width)] * splits

    early, late = early_offsets(splits)

    def wide(*shape):
        return [pltpu.VMEM(shape, jnp.bfloat16)] * 2

    inside, anywhere = pl.BlockSpec(memory_space=pltpu.VMEM), pl.BlockSpec(memory_space=pl.ANY)
    pair = pl.pallas_call(
        pack_kernel,
        name="pack",
        out_shape=f32(2 * own, width),
        in_specs=[anywhere] * 2,
        out_specs=inside,
        scratch_shapes=[pltpu.SemaphoreType.DMA((2,))],
        compiler_params=pltpu.CompilerParams(vmem_limit_bytes=60 * 1024 * 1024),
    )(branch_first, branch_second)
    ring = Ring(pair)
    ring.step()
    cotan_far = swap(cotan_rows, 2)
    near, away = call(
        functools.partial(pick_kernel, groups),
        "pick",
        [f32(2 * height, low)] * 2,
        2 * unit,
        [],
        stem_rows,
        ordered(first_bond, pair),
    )
    near, away = ring.after(near, away)
    ring.step()
    pieces = dict(enumerate(ring.pieces))
    cotan_far, near, away = ring.after(cotan_far, near, away)
    ring.step()
    away = swap(away, 2)
    near_back, cotan_high, cotan_low = call(
        functools.partial(early_back_kernel, groups, own),
        "early_back",
        [f32(len(early) * own, tall)] + [b16(tall, width)] * 2,
        3 * unit * len(early) // splits,
        wide(len(early) * own, width),
        cotan_rows,
        swap(cotan_rows, 1),
        cotan_far,
        swap(cotan_far, 1),
        *[pieces[k] for k in early],
    )
    near_far = swap(near_back, 2)
    near, away, _ = ring.after(near, away, near_back)
    for _ in range(ring.size // 2 - 3):
        ring.step()
    picked = near, swap(near, 1), away, swap(away, 1)
    cotan_high, near_far, *picked = lax.optimization_barrier((cotan_high, near_far, *picked))
    far = splits // 2
    pieces_first = ring.pieces[: far + 1] + ring.pieces[far + 2 :]
    pieces_second = ring.pieces[:far] + ring.pieces[far + 1 :]
    far_back = call(
        functools.partial(late_back_kernel, own),
        "late_back",
        [f32(len(late) * own, tall)],
        3 * unit * len(late) // splits,
        wide(len(late) * own, width),
        cotan_high,
        cotan_low,
        *[pieces_second[k] for k in late],
    )[0]
    far_far = swap(far_back, 2)
    *mid, first_high, first_low = call(
        functools.partial(mid_kernel, groups),
        "mid",
        [f32(2 * tall, low)] * 2 + [b16(low, width)] * 2,
        3 * unit + 2 * groups * unit,
        wide(tall, width),
        ordered(second_bond, far_back),
        *picked,
        *pieces_first,
    )
    mid[1], far_far = lax.optimization_barrier((mid[1], far_far))
    mid = mid[0] + swap(mid[1], 1)
    near_mid, away_mid, far_far, near_far = lax.optimization_barrier((mid[:tall], mid[tall:], far_far, near_far))
    regrouped = [near_mid, swap(away_mid, 2)]
    gathered = [
        [near_back, swap(near_back, 1), near_far, swap(near_far, 1)],
        [far_back, swap(far_back, 1), far_far, swap(far_far, 1)],
    ]
    *outer_first, turned_high, turned_low = call(
        functools.partial(first_kernel, groups, factor),
        "grad_first",
        blocks + [b16(width, tall)] * 2,
        3 * unit + 2 * groups * unit,
        wide(width, tall) + wide(low, tall) + [pltpu.VMEM((low, width), jnp.float32)],
        second_bond,
        *gathered[0],
        *gathered[1],
        *picked,
    )
    outer = call(
        functools.partial(second_kernel, factor),
        "grad_second",
        [f32(2 * own, width)] * splits,
        3 * unit,
        [pltpu.VMEM((low, width), jnp.float32)],
        *regrouped,
        cotan_high,
        cotan_low,
        *outer_first,
    )
    grad = call(
        functools.partial(stem_kernel, groups),
        "grad_stem",
        [f32(2 * low, height)] * 2,
        3 * unit,
        [pltpu.VMEM((low, tall), jnp.float32)],
        ordered(first_high, outer[0]),
        first_low,
        turned_high,
        turned_low,
    )
    moved = pair_exchange(*grad)
    placed = call(place_kernel, "place", [f32(height, width)], 2 * unit, [], first_bond, *moved)[0]
    grads = gy_reduce(outer, {1: grad, 2: moved, 3: (placed,)})
    return placed.reshape(1, height, width), grads[:own], grads[own:]


def solution(mesh):
    return jax.shard_map(
        on_device,
        mesh=mesh,
        in_specs=(
            P("gx", "gy", None),
            P("gx", "gy", None),
            P(("gx", "gy"), None),
            P(("gx", "gy"), None),
            P(),
            P(),
        ),
        out_specs=(P("gx", "gy", None), P(("gx", "gy"), None), P(("gx", "gy"), None)),
        check_vma=False,
    )
```

```python
import functools

import jax
import jax.numpy as jnp
from jax import lax
from jax.experimental import pallas as pl
from jax.experimental.pallas import tpu as pltpu
from jax.sharding import PartitionSpec as P


def product(left, right, contract):
    return lax.dot_general(
        left,
        right,
        (contract, ((), ())),
        precision=lax.Precision.HIGH,
        preferred_element_type=jnp.float32,
    )


def inverse(ordering):
    return jnp.zeros_like(ordering).at[ordering].set(jnp.arange(ordering.shape[0], dtype=jnp.int32))


def swap(block, mask):
    size = lax.axis_size("gx")
    return lax.ppermute(block, "gx", [(i, i ^ mask) for i in range(size)])


def masks(size):
    return [1 << bit for bit in range(size.bit_length() - 1)]


def gx_gather(block):
    held = {0: block}
    for mask in reversed(masks(lax.axis_size("gx"))):
        held.update({rel ^ mask: swap(held[rel], mask) for rel in list(held)})
    return [held[rel] for rel in range(len(held))]


def gx_reduce(blocks):
    held = dict(enumerate(blocks))
    for mask in masks(lax.axis_size("gx")):
        held = {rel: held[rel] + swap(held[rel ^ mask], mask) for rel in held if not rel & mask}
    return held[0]


def gx_exchange(blocks):
    return [block if rel == 0 else swap(block, rel) for rel, block in enumerate(blocks)]


def pair_exchange(near, away):
    away = swap(away, 2)
    return near, swap(near, 1), away, swap(away, 1)


def pair_blocks(refs):
    half = refs[0].shape[0] // 2
    return [ref[half:] if rel % 2 else ref[:half] for rel, ref in enumerate(refs)]


def ring_order(size):
    return [i for i in range(size) if i % 2 == 0] + [i for i in reversed(range(size)) if i % 2]


def ring_step(block, step):
    order = ring_order(lax.axis_size("gy"))
    size = len(order)
    return lax.ppermute(block, "gy", [(order[k], order[(k + step) % size]) for k in range(size)])


def ordered(value, *others):
    return lax.optimization_barrier((value, *others))[0]


class Ring:
    def __init__(self, block):
        self.size = lax.axis_size("gy")
        self.ahead = self.behind = block
        self.taken = 0
        self.last = []
        self.pieces = [block] + [None] * (self.size - 1)

    def after(self, *others):
        self.ahead, self.behind, *others = lax.optimization_barrier((self.ahead, self.behind, *others))
        return others

    def step(self):
        self.taken += 1
        if self.taken < self.size // 2:
            self.ahead, self.behind = ring_step(self.ahead, -1), ring_step(self.behind, 1)
            self.pieces[self.taken], self.pieces[self.size - self.taken] = self.ahead, self.behind
            self.last.append((self.ahead, self.behind))
            return
        half = self.ahead.shape[0] // 2
        halves = [ring_step(self.ahead[:half], -1), ring_step(self.behind[half:], 1)]
        self.pieces[self.taken : self.taken + 1] = halves


def gy_pieces(block):
    ring = Ring(block)
    for _ in range(ring.size // 2):
        ring.step()
    return ring.pieces


def gy_gather(block):
    return jnp.concatenate(gy_pieces(block), axis=0)


class RingSum:
    def __init__(self, blocks):
        self.size = len(blocks)
        self.left = self.size // 2
        self.blocks = blocks
        self.half = blocks[0].shape[0] // 2
        far = blocks[self.left]
        self.ahead, self.behind = far[: self.half], far[self.half :]
        self.total = None

    def after(self, *others):
        self.ahead, self.behind, *others = lax.optimization_barrier((self.ahead, self.behind, *others))
        return others

    def step(self):
        ahead, behind = ring_step(self.ahead, 1), ring_step(self.behind, -1)
        self.left -= 1
        if not self.left:
            self.total = self.blocks[0] + ahead + behind
            return
        near, back = self.blocks[self.left], self.blocks[self.size - self.left]
        if ahead.shape[0] == self.half:
            ahead = jnp.concatenate([near[: self.half] + ahead, near[self.half :]], axis=0)
            behind = jnp.concatenate([back[: self.half], back[self.half :] + behind], axis=0)
            self.ahead, self.behind = ahead, behind
        else:
            self.ahead, self.behind = near + ahead, back + behind


def gy_reduce(blocks):
    ring = RingSum(blocks)
    for _ in range(ring.size // 2):
        ring.step()
    return ring.total


def plain(stem_first, cotangent, branch_first, branch_second, bond_first, bond_second):
    groups, splits = lax.axis_size("gx"), lax.axis_size("gy")
    me_x, me_y = lax.axis_index("gx"), lax.axis_index("gy")
    height, width = stem_first.shape[1:]
    low = width // groups
    own = width // (groups * splits)
    factor = 1.0 / jnp.sqrt(jnp.float32(height * groups * splits))
    stem_rows = stem_first.reshape(height, width)
    cotan_rows = cotangent.reshape(height, width)

    partner = me_x ^ jnp.arange(groups, dtype=jnp.int32)
    order = jnp.array(ring_order(splits), jnp.int32)
    place = jnp.zeros_like(order).at[order].set(jnp.arange(splits, dtype=jnp.int32))
    ahead = order[(place[me_y] + jnp.arange(splits, dtype=jnp.int32)) % splits]
    rows = (
        partner[:, None, None] * low + ahead[None, :, None] * own + jnp.arange(own, dtype=jnp.int32)[None, None, :]
    ).reshape(width)
    bond_first, bond_second = bond_first[rows], bond_second[rows]
    bond_second = ((bond_second // low) ^ me_x) * low + bond_second % low
    back_first, back_second = inverse(bond_first), inverse(bond_second)

    block_first, block_second = gy_gather(branch_first), gy_gather(branch_second)
    cotan_all = jnp.concatenate(gx_gather(cotan_rows), axis=0)
    picked = jnp.take(stem_rows, bond_first, axis=1)
    picked = gx_exchange([picked[:, rel * low : (rel + 1) * low] for rel in range(groups)])
    picked = jnp.concatenate(picked, axis=0)

    mid = product(picked, block_first, ((1,), (0,)))
    mid = mid.reshape(groups, height, groups, low).transpose(2, 1, 0, 3).reshape(groups * height, width)
    mid = jnp.take(mid, bond_second, axis=1)
    regrouped = gx_reduce([mid[:, rel * low : (rel + 1) * low] for rel in range(groups)])
    regrouped = regrouped.reshape(groups, height, low)[partner].reshape(groups * height, low)
    outer_second = product(regrouped, cotan_all, ((0,), (0,)))
    grad_second = gy_reduce([outer_second[k * own : (k + 1) * own] for k in range(splits)])

    back = product(cotan_all, block_second, ((1,), (1,)))
    pieces = gx_gather(back)
    pieces = [
        jnp.concatenate([piece.reshape(groups, height, low)[h ^ rel] for h in range(groups)], axis=0)
        for rel, piece in enumerate(pieces)
    ]
    back_mid = jnp.take(jnp.concatenate(pieces, axis=1), back_second, axis=1)
    back_mid = back_mid.reshape(groups, height, groups, low).transpose(2, 1, 0, 3).reshape(groups * height, width)

    outer_first = product(picked, back_mid, ((0,), (0,)))
    grad_first = gy_reduce([outer_first[k * own : (k + 1) * own] for k in range(splits)])
    grad_first = grad_first.reshape(own, groups, low)[:, partner].reshape(own, width)

    turned = block_first.reshape(low, groups, low)[:, partner].reshape(low, width)
    grad = product(back_mid, turned, ((1,), (1,)))
    grad = gx_exchange([grad[rel * height : (rel + 1) * height] for rel in range(groups)])
    grad_stem = jnp.take(jnp.concatenate(grad, axis=1), back_first, axis=1).reshape(1, height, width)
    return (grad_stem, grad_first * factor, grad_second * factor)


def split(value):
    high = value.astype(jnp.bfloat16)
    return high, (value - high.astype(jnp.float32)).astype(jnp.bfloat16)


def dot(left, right, contract):
    return lax.dot_general(left, right, (contract, ((), ())), preferred_element_type=jnp.float32)


def dot_parts(left, right, contract):
    return dot(left[0], right[0], contract) + dot(left[0], right[1], contract) + dot(left[1], right[0], contract)


def ring_owner(offset):
    size = lax.axis_size("gy")
    me = lax.axis_index("gy")
    place = jnp.where(me % 2 == 0, me // 2, size - 1 - me // 2)
    place = (place + offset) % size
    return jnp.where(place < size // 2, 2 * place, 2 * (size - 1 - place) + 1)


def group(rel):
    return lax.axis_index("gx") ^ rel


def early_offsets(size):
    near = [k for k in range(size) if min(k, size - k) <= min(2, size // 4)]
    return near, [k for k in range(size) if k not in near]


def aligned(index, size):
    return pl.ds(pl.multiple_of(index * size, size), size)


def store_split(high_ref, low_ref, where, value):
    high_ref[where], low_ref[where] = split(value)


def branch_rows(ref, own, part):
    return ref[...] if ref.shape[0] == own else ref[part * own : (part + 1) * own]


def chosen(bond_ref, rel, low, width):
    columns = bond_ref[:, aligned(group(rel), low)]
    position = lax.broadcasted_iota(jnp.int32, (width, low), 0)
    return (position == columns).astype(jnp.bfloat16)


def put_pairs(blocks, pair_refs):
    size = pair_refs[0].shape[0] // 2
    for rel, block in enumerate(blocks):
        pair_refs[rel // 2][rel % 2 * size : (rel % 2 + 1) * size] = block


def pack_kernel(*refs):
    ahead, behind = refs[4:]
    own = refs[0].shape[0]
    for part, (ahead_ref, behind_ref) in enumerate((refs[:2], refs[2:4])):
        ahead[part * own : (part + 1) * own] = ahead_ref[...]
        behind[part * own : (part + 1) * own] = behind_ref[...]


def pick_kernel(groups, stem_ref, bond_ref, *out_refs):
    high, low_part = split(stem_ref[...])
    width = stem_ref.shape[1]
    selects = [chosen(bond_ref, rel, width // groups, width) for rel in range(groups)]
    put_pairs([dot(high, one, ((1,), (0,))) + dot(low_part, one, ((1,), (0,))) for one in selects], out_refs)


def absorb(picked, branch, mid, groups):
    height, low = picked[0].shape[0] // 2, picked[0].shape[1]
    for rel, block in enumerate(pair_blocks(picked)):
        parts = split(block)
        columns = aligned(group(rel), low)
        for h in range(groups):
            cut = slice(h * low, (h + 1) * low)
            value = dot_parts(parts, (branch[0][:, cut], branch[1][:, cut]), ((1,), (0,)))
            store_split(*mid, (slice(h * height, (h + 1) * height), columns), value)


def put_picks(bond_ref, mid, out_ref, side):
    rows, width = mid[0].shape
    low = out_ref.shape[1]
    for part in range(2):
        select = chosen(bond_ref, 2 * part + side, low, width)
        block = dot(mid[0][...], select, ((1,), (0,))) + dot(mid[1][...], select, ((1,), (0,)))
        out_ref[part * rows : (part + 1) * rows] = block


def mid_kernel(groups, bond_ref, *refs):
    picked, refs = refs[:groups], refs[groups:]
    out_ref, branch, mid = refs[-5], refs[-4:-2], refs[-2:]
    own = branch[0].shape[0] // lax.axis_size("gy")
    for k, ref in enumerate(refs[:-5]):
        store_split(*branch, aligned(ring_owner(k), own), branch_rows(ref, own, 0))
    absorb(picked, branch, mid, groups)
    put_picks(bond_ref, mid, out_ref, 1)


def rest_kernel(bond_ref, mid_high, mid_low, out_ref):
    put_picks(bond_ref, (mid_high, mid_low), out_ref, 0)


def gather_rows(pieces, rows, own):
    for k, ref in enumerate(pieces):
        store_split(*rows, slice(k * own, (k + 1) * own), branch_rows(ref, own, 1))


def early_back_kernel(groups, own, *refs):
    cotan, refs = refs[:groups], refs[groups:]
    pieces, (out_ref, cotan_high, cotan_low, *rows) = refs[:-5], refs[-5:]
    height = cotan[0].shape[0]
    gather_rows(pieces, rows, own)
    for rel, ref in enumerate(cotan):
        store_split(cotan_high, cotan_low, aligned(group(rel), height), ref[...])
    out_ref[...] = dot_parts((rows[0][...], rows[1][...]), (cotan_high[...], cotan_low[...]), ((1,), (1,)))


def late_back_kernel(own, cotan_high, cotan_low, *refs):
    pieces, (out_ref, *rows) = refs[:-3], refs[-3:]
    gather_rows(pieces, rows, own)
    out_ref[...] = dot_parts((rows[0][...], rows[1][...]), (cotan_high[...], cotan_low[...]), ((1,), (1,)))


def put_blocks(total, out_refs, total_ref):
    own = out_refs[0].shape[0]
    total_ref[...] = total
    for k, out_ref in enumerate(out_refs):
        out_ref[...] = total_ref[aligned(ring_owner(k), own)]


def second_kernel(factor, near_ref, far_ref, cotan_high, cotan_low, *refs):
    firsts, refs = refs[: (len(refs) - 1) // 2], refs[(len(refs) - 1) // 2 :]
    out_refs, total_ref = refs[:-1], refs[-1]
    own = firsts[0].shape[0]
    parts = split(((near_ref[...] + far_ref[...]) * factor).T)
    total_ref[...] = dot_parts(parts, (cotan_high[...], cotan_low[...]), ((1,), (0,)))
    for k, (ref, out_ref) in enumerate(zip(firsts, out_refs, strict=True)):
        out_ref[:own] = ref[...]
        out_ref[own:] = total_ref[aligned(ring_owner(k), own)]


def first_kernel(groups, factor, bond_ref, *refs):
    near, far, picked, refs = refs[:groups], refs[groups : 2 * groups], refs[2 * groups : 3 * groups], refs[3 * groups :]
    out_refs, (turned_high, turned_low, rows_high, rows_low, picked_high, picked_low, total_ref) = refs[:-7], refs[-7:]
    height, low = picked[0].shape[0] // 2, picked[0].shape[1]
    width = groups * low
    size = lax.axis_size("gy")
    own = low // size
    for pieces, offsets in zip((near, far), early_offsets(size)):
        for rel, ref in enumerate(pieces):
            for number, k in enumerate(offsets):
                where = aligned(group(rel) * size + ring_owner(k), own)
                store_split(rows_high, rows_low, where, ref[number * own : (number + 1) * own])
    position = lax.broadcasted_iota(jnp.int32, (width, width), 0)
    select = (position == bond_ref[...]).astype(jnp.bfloat16)
    total = dot(select, rows_high[...], ((1,), (0,))) + dot(select, rows_low[...], ((1,), (0,)))
    for h in range(groups):
        for a in range(groups):
            value = total[a * low : (a + 1) * low, h * height : (h + 1) * height]
            where = (slice(h * low, (h + 1) * low), slice(a * height, (a + 1) * height))
            store_split(turned_high, turned_low, where, value)
    for rel, block in enumerate(pair_blocks(picked)):
        store_split(picked_high, picked_low, (slice(None), aligned(group(rel), height)), (block * factor).T)
    parts = picked_high[...], picked_low[...]
    put_blocks(dot_parts(parts, (turned_high[...], turned_low[...]), ((1,), (1,))), out_refs, total_ref)


def stem_kernel(groups, branch_high, branch_low, turned_high, turned_low, *refs):
    out_refs, total_ref = refs[:-1], refs[-1]
    height = total_ref.shape[1] // groups
    branch, turned = (branch_high[...], branch_low[...]), (turned_high[...], turned_low[...])
    total_ref[...] = dot_parts(branch, turned, ((1,), (0,)))
    put_pairs([total_ref[:, aligned(group(rel), height)] for rel in range(groups)], out_refs)


def place_kernel(bond_ref, *refs):
    blocks, out_ref = refs[:-1], refs[-1]
    total = None
    for rel, block in enumerate(pair_blocks(blocks)):
        select = chosen(bond_ref, rel, block.shape[0], out_ref.shape[1])
        high, low_part = split(block.T)
        term = dot(high, select, ((1,), (1,))) + dot(low_part, select, ((1,), (1,)))
        total = term if total is None else total + term
    out_ref[...] = total


def call(kernel, name, outs, flops, scratch, *operands):
    moved = sum(x.size * x.dtype.itemsize for x in (*operands, *outs))
    whole = pl.BlockSpec(memory_space=pltpu.VMEM)
    return pl.pallas_call(
        kernel,
        name=name,
        out_shape=outs,
        in_specs=[whole] * len(operands),
        out_specs=[whole] * len(outs),
        scratch_shapes=scratch,
        compiler_params=pltpu.CompilerParams(vmem_limit_bytes=32 * 1024 * 1024),
        cost_estimate=pl.CostEstimate(flops=flops, bytes_accessed=moved, transcendentals=0),
    )(*operands)


def f32(*shape):
    return jax.ShapeDtypeStruct(shape, jnp.float32)


def b16(*shape):
    return jax.ShapeDtypeStruct(shape, jnp.bfloat16)


def on_device(stem_first, cotangent, branch_first, branch_second, bond_first, bond_second):
    groups, splits = lax.axis_size("gx"), lax.axis_size("gy")
    height, width = stem_first.shape[1:]
    low = width // groups
    own = width // (groups * splits)
    if groups != 4 or splits % 2 or splits < 8 or low % 128 or own % 32 or height % 128:
        return plain(stem_first, cotangent, branch_first, branch_second, bond_first, bond_second)
    factor = (height * groups * splits) ** -0.5
    tall = groups * height
    unit = 2 * height * width * width
    first_bond, second_bond = bond_first.reshape(1, width), bond_second.reshape(1, width)
    stem_rows, cotan_rows = stem_first.reshape(height, width), cotangent.reshape(height, width)
    blocks = [f32(own, width)] * splits

    early, late = early_offsets(splits)

    def wide(*shape):
        return [pltpu.VMEM(shape, jnp.bfloat16)] * 2

    neighbours = [ring_step(branch, step) for branch in (branch_first, branch_second) for step in (-1, 1)]
    cotan_far = swap(cotan_rows, 2)
    ring = Ring(None)
    ring.taken = 1
    near, away = call(
        functools.partial(pick_kernel, groups),
        "pick",
        [f32(2 * height, low)] * 2,
        2 * unit,
        [],
        stem_rows,
        first_bond,
    )
    ring.ahead, ring.behind = call(pack_kernel, "pack", [f32(2 * own, width)] * 2, 0, [], *neighbours)
    ring.pieces[1], ring.pieces[-1] = ring.ahead, ring.behind
    near, away = ring.after(near, away)
    ring.step()
    ring.pieces[0] = branch_second
    pieces = dict(enumerate(ring.pieces))
    away = swap(away, 2)
    cotan_far, near, away = ring.after(cotan_far, near, away)
    ring.step()
    near_back, cotan_high, cotan_low = call(
        functools.partial(early_back_kernel, groups, own),
        "early_back",
        [f32(len(early) * own, tall)] + [b16(tall, width)] * 2,
        3 * unit * len(early) // splits,
        wide(len(early) * own, width),
        cotan_rows,
        swap(cotan_rows, 1),
        cotan_far,
        swap(cotan_far, 1),
        *[pieces[k] for k in early],
    )
    near_far = swap(near_back, 2)
    ring.after(near_back)
    for _ in range(ring.size // 2 - 3):
        ring.step()
    picked = near, swap(near, 1), away, swap(away, 1)
    cotan_high, near_far, *picked = lax.optimization_barrier((cotan_high, near_far, *picked))
    far = splits // 2
    pieces_first = [branch_first] + ring.pieces[1 : far + 1] + ring.pieces[far + 2 :]
    pieces_second = ring.pieces[:far] + ring.pieces[far + 1 :]
    far_back = call(
        functools.partial(late_back_kernel, own),
        "late_back",
        [f32(len(late) * own, tall)],
        3 * unit * len(late) // splits,
        wide(len(late) * own, width),
        cotan_high,
        cotan_low,
        *[pieces_second[k] for k in late],
    )[0]
    far_far = swap(far_back, 2)
    across, first_high, first_low, mid_high, mid_low = call(
        functools.partial(mid_kernel, groups),
        "mid",
        [f32(2 * tall, low)] + [b16(low, width)] * 2 + [b16(tall, width)] * 2,
        3 * unit + groups * unit,
        [],
        ordered(second_bond, far_back),
        *picked,
        *pieces_first,
    )
    beside = call(rest_kernel, "rest", [f32(2 * tall, low)], 50 * groups * unit, [], ordered(second_bond, far_far), mid_high, mid_low)[0]
    mid = beside + swap(across, 1)
    near_mid, away_mid, near_far = lax.optimization_barrier((mid[:tall], mid[tall:], near_far))
    regrouped = [near_mid, swap(away_mid, 2)]
    gathered = [
        [near_back, swap(near_back, 1), near_far, swap(near_far, 1)],
        [far_back, swap(far_back, 1), far_far, swap(far_far, 1)],
    ]
    *outer_first, turned_high, turned_low = call(
        functools.partial(first_kernel, groups, factor),
        "grad_first",
        blocks + [b16(width, tall)] * 2,
        3 * unit + 2 * groups * unit,
        wide(width, tall) + wide(low, tall) + [pltpu.VMEM((low, width), jnp.float32)],
        second_bond,
        *gathered[0],
        *gathered[1],
        *picked,
    )
    grad = call(
        functools.partial(stem_kernel, groups),
        "grad_stem",
        [f32(2 * low, height)] * 2,
        3 * unit,
        [pltpu.VMEM((low, tall), jnp.float32)],
        first_high,
        first_low,
        turned_high,
        turned_low,
    )
    *grad, regrouped[0] = lax.optimization_barrier((*grad, regrouped[0]))
    outer = call(
        functools.partial(second_kernel, factor),
        "grad_second",
        [f32(2 * own, width)] * splits,
        3 * unit,
        [pltpu.VMEM((low, width), jnp.float32)],
        *regrouped,
        cotan_high,
        cotan_low,
        *outer_first,
    )
    sums = RingSum(outer)
    sums.step()
    grad = sums.after(*grad)
    sums.step()
    for _ in range(far - 3):
        sums.step()
    moved = sums.after(*pair_exchange(*grad))
    sums.step()
    placed = call(place_kernel, "place", [f32(height, width)], 2 * unit, [], first_bond, *moved)[0]
    return placed.reshape(1, height, width), sums.total[:own], sums.total[own:]


def solution(mesh):
    return jax.shard_map(
        on_device,
        mesh=mesh,
        in_specs=(
            P("gx", "gy", None),
            P("gx", "gy", None),
            P(("gx", "gy"), None),
            P(("gx", "gy"), None),
            P(),
            P(),
        ),
        out_specs=(P("gx", "gy", None), P(("gx", "gy"), None), P(("gx", "gy"), None)),
        check_vma=False,
    )
```

```python
import functools

import jax
import jax.numpy as jnp
from jax import lax
from jax.experimental import pallas as pl
from jax.experimental.pallas import tpu as pltpu
from jax.sharding import PartitionSpec as P


def product(left, right, contract):
    return lax.dot_general(
        left,
        right,
        (contract, ((), ())),
        precision=lax.Precision.HIGH,
        preferred_element_type=jnp.float32,
    )


def inverse(ordering):
    return jnp.zeros_like(ordering).at[ordering].set(jnp.arange(ordering.shape[0], dtype=jnp.int32))


def swap(block, mask):
    size = lax.axis_size("gx")
    return lax.ppermute(block, "gx", [(i, i ^ mask) for i in range(size)])


def masks(size):
    return [1 << bit for bit in range(size.bit_length() - 1)]


def gx_gather(block):
    held = {0: block}
    for mask in reversed(masks(lax.axis_size("gx"))):
        held.update({rel ^ mask: swap(held[rel], mask) for rel in list(held)})
    return [held[rel] for rel in range(len(held))]


def gx_reduce(blocks):
    held = dict(enumerate(blocks))
    for mask in masks(lax.axis_size("gx")):
        held = {rel: held[rel] + swap(held[rel ^ mask], mask) for rel in held if not rel & mask}
    return held[0]


def gx_exchange(blocks):
    return [block if rel == 0 else swap(block, rel) for rel, block in enumerate(blocks)]


def pair_exchange(near, away):
    away = swap(away, 2)
    return near, swap(near, 1), away, swap(away, 1)


def pair_blocks(refs):
    half = refs[0].shape[0] // 2
    return [ref[half:] if rel % 2 else ref[:half] for rel, ref in enumerate(refs)]


def ring_order(size):
    return [i for i in range(size) if i % 2 == 0] + [i for i in reversed(range(size)) if i % 2]


def ring_step(block, step):
    order = ring_order(lax.axis_size("gy"))
    size = len(order)
    return lax.ppermute(block, "gy", [(order[k], order[(k + step) % size]) for k in range(size)])


def ordered(value, *others):
    return lax.optimization_barrier((value, *others))[0]


class Ring:
    def __init__(self, block):
        self.size = lax.axis_size("gy")
        self.ahead = self.behind = block
        self.taken = 0
        self.last = []
        self.pieces = [block] + [None] * (self.size - 1)

    def after(self, *others):
        self.ahead, self.behind, *others = lax.optimization_barrier((self.ahead, self.behind, *others))
        return others

    def step(self):
        self.taken += 1
        if self.taken < self.size // 2:
            self.ahead, self.behind = ring_step(self.ahead, -1), ring_step(self.behind, 1)
            self.pieces[self.taken], self.pieces[self.size - self.taken] = self.ahead, self.behind
            self.last.append((self.ahead, self.behind))
            return
        half = self.ahead.shape[0] // 2
        halves = [ring_step(self.ahead[:half], -1), ring_step(self.behind[half:], 1)]
        self.pieces[self.taken : self.taken + 1] = halves


def gy_pieces(block):
    ring = Ring(block)
    for _ in range(ring.size // 2):
        ring.step()
    return ring.pieces


def gy_gather(block):
    return jnp.concatenate(gy_pieces(block), axis=0)


class RingSum:
    def __init__(self, blocks):
        self.size = len(blocks)
        self.left = self.size // 2
        self.blocks = blocks
        self.half = blocks[0].shape[0] // 2
        far = blocks[self.left]
        self.ahead, self.behind = far[: self.half], far[self.half :]
        self.total = None

    def after(self, *others):
        self.ahead, self.behind, *others = lax.optimization_barrier((self.ahead, self.behind, *others))
        return others

    def step(self):
        ahead, behind = ring_step(self.ahead, 1), ring_step(self.behind, -1)
        self.left -= 1
        if not self.left:
            self.total = self.blocks[0] + ahead + behind
            return
        near, back = self.blocks[self.left], self.blocks[self.size - self.left]
        if ahead.shape[0] == self.half:
            ahead = jnp.concatenate([near[: self.half] + ahead, near[self.half :]], axis=0)
            behind = jnp.concatenate([back[: self.half], back[self.half :] + behind], axis=0)
            self.ahead, self.behind = ahead, behind
        else:
            self.ahead, self.behind = near + ahead, back + behind


def gy_reduce(blocks):
    ring = RingSum(blocks)
    for _ in range(ring.size // 2):
        ring.step()
    return ring.total


def plain(stem_first, cotangent, branch_first, branch_second, bond_first, bond_second):
    groups, splits = lax.axis_size("gx"), lax.axis_size("gy")
    me_x, me_y = lax.axis_index("gx"), lax.axis_index("gy")
    height, width = stem_first.shape[1:]
    low = width // groups
    own = width // (groups * splits)
    factor = 1.0 / jnp.sqrt(jnp.float32(height * groups * splits))
    stem_rows = stem_first.reshape(height, width)
    cotan_rows = cotangent.reshape(height, width)

    partner = me_x ^ jnp.arange(groups, dtype=jnp.int32)
    order = jnp.array(ring_order(splits), jnp.int32)
    place = jnp.zeros_like(order).at[order].set(jnp.arange(splits, dtype=jnp.int32))
    ahead = order[(place[me_y] + jnp.arange(splits, dtype=jnp.int32)) % splits]
    rows = (
        partner[:, None, None] * low + ahead[None, :, None] * own + jnp.arange(own, dtype=jnp.int32)[None, None, :]
    ).reshape(width)
    bond_first, bond_second = bond_first[rows], bond_second[rows]
    bond_second = ((bond_second // low) ^ me_x) * low + bond_second % low
    back_first, back_second = inverse(bond_first), inverse(bond_second)

    block_first, block_second = gy_gather(branch_first), gy_gather(branch_second)
    cotan_all = jnp.concatenate(gx_gather(cotan_rows), axis=0)
    picked = jnp.take(stem_rows, bond_first, axis=1)
    picked = gx_exchange([picked[:, rel * low : (rel + 1) * low] for rel in range(groups)])
    picked = jnp.concatenate(picked, axis=0)

    mid = product(picked, block_first, ((1,), (0,)))
    mid = mid.reshape(groups, height, groups, low).transpose(2, 1, 0, 3).reshape(groups * height, width)
    mid = jnp.take(mid, bond_second, axis=1)
    regrouped = gx_reduce([mid[:, rel * low : (rel + 1) * low] for rel in range(groups)])
    regrouped = regrouped.reshape(groups, height, low)[partner].reshape(groups * height, low)
    outer_second = product(regrouped, cotan_all, ((0,), (0,)))
    grad_second = gy_reduce([outer_second[k * own : (k + 1) * own] for k in range(splits)])

    back = product(cotan_all, block_second, ((1,), (1,)))
    pieces = gx_gather(back)
    pieces = [
        jnp.concatenate([piece.reshape(groups, height, low)[h ^ rel] for h in range(groups)], axis=0)
        for rel, piece in enumerate(pieces)
    ]
    back_mid = jnp.take(jnp.concatenate(pieces, axis=1), back_second, axis=1)
    back_mid = back_mid.reshape(groups, height, groups, low).transpose(2, 1, 0, 3).reshape(groups * height, width)

    outer_first = product(picked, back_mid, ((0,), (0,)))
    grad_first = gy_reduce([outer_first[k * own : (k + 1) * own] for k in range(splits)])
    grad_first = grad_first.reshape(own, groups, low)[:, partner].reshape(own, width)

    turned = block_first.reshape(low, groups, low)[:, partner].reshape(low, width)
    grad = product(back_mid, turned, ((1,), (1,)))
    grad = gx_exchange([grad[rel * height : (rel + 1) * height] for rel in range(groups)])
    grad_stem = jnp.take(jnp.concatenate(grad, axis=1), back_first, axis=1).reshape(1, height, width)
    return (grad_stem, grad_first * factor, grad_second * factor)


def split(value):
    high = value.astype(jnp.bfloat16)
    return high, (value - high.astype(jnp.float32)).astype(jnp.bfloat16)


def dot(left, right, contract):
    return lax.dot_general(left, right, (contract, ((), ())), preferred_element_type=jnp.float32)


def dot_parts(left, right, contract):
    return dot(left[0], right[0], contract) + dot(left[0], right[1], contract) + dot(left[1], right[0], contract)


def ring_owner(offset):
    size = lax.axis_size("gy")
    me = lax.axis_index("gy")
    place = jnp.where(me % 2 == 0, me // 2, size - 1 - me // 2)
    place = (place + offset) % size
    return jnp.where(place < size // 2, 2 * place, 2 * (size - 1 - place) + 1)


def group(rel):
    return lax.axis_index("gx") ^ rel


def early_offsets(size):
    near = [k for k in range(size) if min(k, size - k) <= min(2, size // 4)]
    return near, [k for k in range(size) if k not in near]


def aligned(index, size):
    return pl.ds(pl.multiple_of(index * size, size), size)


def store_split(high_ref, low_ref, where, value):
    high_ref[where], low_ref[where] = split(value)


def branch_rows(ref, own, part):
    return ref[...] if ref.shape[0] == own else ref[part * own : (part + 1) * own]


def chosen(bond_ref, rel, low, width):
    columns = bond_ref[:, aligned(group(rel), low)]
    position = lax.broadcasted_iota(jnp.int32, (width, low), 0)
    return (position == columns).astype(jnp.bfloat16)


def put_pairs(blocks, pair_refs):
    size = pair_refs[0].shape[0] // 2
    for rel, block in enumerate(blocks):
        pair_refs[rel // 2][rel % 2 * size : (rel % 2 + 1) * size] = block


def pack_kernel(*refs):
    ahead, behind = refs[4:]
    own = refs[0].shape[0]
    for part, (ahead_ref, behind_ref) in enumerate((refs[:2], refs[2:4])):
        ahead[part * own : (part + 1) * own] = ahead_ref[...]
        behind[part * own : (part + 1) * own] = behind_ref[...]


def pick_kernel(groups, stem_ref, bond_ref, *out_refs):
    high, low_part = split(stem_ref[...])
    width = stem_ref.shape[1]
    selects = [chosen(bond_ref, rel, width // groups, width) for rel in range(groups)]
    put_pairs([dot(high, one, ((1,), (0,))) + dot(low_part, one, ((1,), (0,))) for one in selects], out_refs)


def absorb(picked, branch, mid, groups):
    height, low = picked[0].shape[0] // 2, picked[0].shape[1]
    for rel, block in enumerate(pair_blocks(picked)):
        parts = split(block)
        columns = aligned(group(rel), low)
        for h in range(groups):
            cut = slice(h * low, (h + 1) * low)
            value = dot_parts(parts, (branch[0][:, cut], branch[1][:, cut]), ((1,), (0,)))
            store_split(*mid, (slice(h * height, (h + 1) * height), columns), value)


def picks(bond_ref, mid, rel, low):
    select = chosen(bond_ref, rel, low, mid[0].shape[1])
    return dot(mid[0][...], select, ((1,), (0,))) + dot(mid[1][...], select, ((1,), (0,)))


def mid_kernel(groups, bond_ref, *refs):
    picked, refs = refs[:groups], refs[groups:]
    out_ref, branch, mid = refs[-5], refs[-4:-2], refs[-2:]
    own = branch[0].shape[0] // lax.axis_size("gy")
    for k, ref in enumerate(refs[:-5]):
        store_split(*branch, aligned(ring_owner(k), own), branch_rows(ref, own, 0))
    absorb(picked, branch, mid, groups)
    out_ref[...] = picks(bond_ref, mid, groups - 1, out_ref.shape[1])


def rest_kernel(partners, bond_ref, mid_high, mid_low, *out_refs):
    for rel, out_ref in zip(partners, out_refs, strict=True):
        out_ref[...] = picks(bond_ref, (mid_high, mid_low), rel, out_ref.shape[1])


def gather_rows(pieces, rows, own):
    for k, ref in enumerate(pieces):
        store_split(*rows, slice(k * own, (k + 1) * own), branch_rows(ref, own, 1))


def early_back_kernel(groups, own, *refs):
    cotan, refs = refs[:groups], refs[groups:]
    pieces, (out_ref, cotan_high, cotan_low, *rows) = refs[:-5], refs[-5:]
    height = cotan[0].shape[0]
    gather_rows(pieces, rows, own)
    for rel, ref in enumerate(cotan):
        store_split(cotan_high, cotan_low, aligned(group(rel), height), ref[...])
    out_ref[...] = dot_parts((rows[0][...], rows[1][...]), (cotan_high[...], cotan_low[...]), ((1,), (1,)))


def late_back_kernel(own, cotan_high, cotan_low, *refs):
    pieces, (out_ref, *rows) = refs[:-3], refs[-3:]
    gather_rows(pieces, rows, own)
    out_ref[...] = dot_parts((rows[0][...], rows[1][...]), (cotan_high[...], cotan_low[...]), ((1,), (1,)))


def put_blocks(total, out_refs, total_ref):
    own = out_refs[0].shape[0]
    total_ref[...] = total
    for k, out_ref in enumerate(out_refs):
        out_ref[...] = total_ref[aligned(ring_owner(k), own)]


def second_kernel(factor, near_ref, beside_ref, far_ref, cotan_high, cotan_low, *refs):
    firsts, refs = refs[: (len(refs) - 1) // 2], refs[(len(refs) - 1) // 2 :]
    out_refs, total_ref = refs[:-1], refs[-1]
    own = firsts[0].shape[0]
    parts = split(((near_ref[...] + beside_ref[...] + far_ref[...]) * factor).T)
    total_ref[...] = dot_parts(parts, (cotan_high[...], cotan_low[...]), ((1,), (0,)))
    for k, (ref, out_ref) in enumerate(zip(firsts, out_refs, strict=True)):
        out_ref[:own] = ref[...]
        out_ref[own:] = total_ref[aligned(ring_owner(k), own)]


def first_kernel(groups, factor, bond_ref, *refs):
    near, far, picked, refs = refs[:groups], refs[groups : 2 * groups], refs[2 * groups : 3 * groups], refs[3 * groups :]
    out_refs, (turned_high, turned_low, rows_high, rows_low, picked_high, picked_low, total_ref) = refs[:-7], refs[-7:]
    height, low = picked[0].shape[0] // 2, picked[0].shape[1]
    width = groups * low
    size = lax.axis_size("gy")
    own = low // size
    for pieces, offsets in zip((near, far), early_offsets(size)):
        for rel, ref in enumerate(pieces):
            for number, k in enumerate(offsets):
                where = aligned(group(rel) * size + ring_owner(k), own)
                store_split(rows_high, rows_low, where, ref[number * own : (number + 1) * own])
    position = lax.broadcasted_iota(jnp.int32, (width, width), 0)
    select = (position == bond_ref[...]).astype(jnp.bfloat16)
    total = dot(select, rows_high[...], ((1,), (0,))) + dot(select, rows_low[...], ((1,), (0,)))
    for h in range(groups):
        for a in range(groups):
            value = total[a * low : (a + 1) * low, h * height : (h + 1) * height]
            where = (slice(h * low, (h + 1) * low), slice(a * height, (a + 1) * height))
            store_split(turned_high, turned_low, where, value)
    for rel, block in enumerate(pair_blocks(picked)):
        store_split(picked_high, picked_low, (slice(None), aligned(group(rel), height)), (block * factor).T)
    parts = picked_high[...], picked_low[...]
    put_blocks(dot_parts(parts, (turned_high[...], turned_low[...]), ((1,), (1,))), out_refs, total_ref)


def stem_kernel(groups, branch_high, branch_low, turned_high, turned_low, *refs):
    out_refs, total_ref = refs[:-1], refs[-1]
    height = total_ref.shape[1] // groups
    branch, turned = (branch_high[...], branch_low[...]), (turned_high[...], turned_low[...])
    total_ref[...] = dot_parts(branch, turned, ((1,), (0,)))
    put_pairs([total_ref[:, aligned(group(rel), height)] for rel in range(groups)], out_refs)


def place_kernel(bond_ref, *refs):
    blocks, out_ref = refs[:-1], refs[-1]
    total = None
    for rel, block in enumerate(pair_blocks(blocks)):
        select = chosen(bond_ref, rel, block.shape[0], out_ref.shape[1])
        high, low_part = split(block.T)
        term = dot(high, select, ((1,), (1,))) + dot(low_part, select, ((1,), (1,)))
        total = term if total is None else total + term
    out_ref[...] = total


def call(kernel, name, outs, flops, scratch, *operands):
    moved = sum(x.size * x.dtype.itemsize for x in (*operands, *outs))
    whole = pl.BlockSpec(memory_space=pltpu.VMEM)
    return pl.pallas_call(
        kernel,
        name=name,
        out_shape=outs,
        in_specs=[whole] * len(operands),
        out_specs=[whole] * len(outs),
        scratch_shapes=scratch,
        compiler_params=pltpu.CompilerParams(vmem_limit_bytes=32 * 1024 * 1024),
        cost_estimate=pl.CostEstimate(flops=flops, bytes_accessed=moved, transcendentals=0),
    )(*operands)


def f32(*shape):
    return jax.ShapeDtypeStruct(shape, jnp.float32)


def b16(*shape):
    return jax.ShapeDtypeStruct(shape, jnp.bfloat16)


def on_device(stem_first, cotangent, branch_first, branch_second, bond_first, bond_second):
    groups, splits = lax.axis_size("gx"), lax.axis_size("gy")
    height, width = stem_first.shape[1:]
    low = width // groups
    own = width // (groups * splits)
    if groups != 4 or splits % 2 or splits < 8 or low % 128 or own % 32 or height % 128:
        return plain(stem_first, cotangent, branch_first, branch_second, bond_first, bond_second)
    factor = (height * groups * splits) ** -0.5
    tall = groups * height
    unit = 2 * height * width * width
    first_bond, second_bond = bond_first.reshape(1, width), bond_second.reshape(1, width)
    stem_rows, cotan_rows = stem_first.reshape(height, width), cotangent.reshape(height, width)
    blocks = [f32(own, width)] * splits

    early, late = early_offsets(splits)

    def wide(*shape):
        return [pltpu.VMEM(shape, jnp.bfloat16)] * 2

    neighbours = [ring_step(branch, step) for branch in (branch_first, branch_second) for step in (-1, 1)]
    cotan_far = swap(cotan_rows, 2)
    ring = Ring(None)
    ring.taken = 1
    near, away = call(
        functools.partial(pick_kernel, groups),
        "pick",
        [f32(2 * height, low)] * 2,
        2 * unit,
        [],
        stem_rows,
        first_bond,
    )
    ring.ahead, ring.behind = call(pack_kernel, "pack", [f32(2 * own, width)] * 2, 0, [], *neighbours)
    ring.pieces[1], ring.pieces[-1] = ring.ahead, ring.behind
    near, away = ring.after(near, away)
    ring.step()
    ring.pieces[0] = branch_second
    pieces = dict(enumerate(ring.pieces))
    away = swap(away, 2)
    cotan_far, near, away = ring.after(cotan_far, near, away)
    ring.step()
    near_back, cotan_high, cotan_low = call(
        functools.partial(early_back_kernel, groups, own),
        "early_back",
        [f32(len(early) * own, tall)] + [b16(tall, width)] * 2,
        3 * unit * len(early) // splits,
        wide(len(early) * own, width),
        cotan_rows,
        swap(cotan_rows, 1),
        cotan_far,
        swap(cotan_far, 1),
        *[pieces[k] for k in early],
    )
    near_far = swap(near_back, 2)
    ring.after(near_back)
    for _ in range(ring.size // 2 - 3):
        ring.step()
    picked = near, swap(near, 1), away, swap(away, 1)
    cotan_high, near_far, *picked = lax.optimization_barrier((cotan_high, near_far, *picked))
    far = splits // 2
    pieces_first = [branch_first] + ring.pieces[1 : far + 1] + ring.pieces[far + 2 :]
    pieces_second = ring.pieces[:far] + ring.pieces[far + 1 :]
    far_back = call(
        functools.partial(late_back_kernel, own),
        "late_back",
        [f32(len(late) * own, tall)],
        3 * unit * len(late) // splits,
        wide(len(late) * own, width),
        cotan_high,
        cotan_low,
        *[pieces_second[k] for k in late],
    )[0]
    far_far = swap(far_back, 2)
    across, first_high, first_low, mid_high, mid_low = call(
        functools.partial(mid_kernel, groups),
        "mid",
        [f32(tall, low)] + [b16(low, width)] * 2 + [b16(tall, width)] * 2,
        3 * unit + unit,
        [],
        ordered(second_bond, far_back),
        *picked,
        *pieces_first,
    )
    away_mid = call(
        functools.partial(rest_kernel, (2,)),
        "across",
        [f32(tall, low)],
        50 * groups * unit,
        [],
        ordered(second_bond, far_far),
        mid_high,
        mid_low,
    )[0]
    away_mid, near_far = lax.optimization_barrier((away_mid + swap(across, 1), near_far))
    gathered = [
        [near_back, swap(near_back, 1), near_far, swap(near_far, 1)],
        [far_back, swap(far_back, 1), far_far, swap(far_far, 1)],
    ]
    *outer_first, turned_high, turned_low = call(
        functools.partial(first_kernel, groups, factor),
        "grad_first",
        blocks + [b16(width, tall)] * 2,
        3 * unit + 2 * groups * unit,
        wide(width, tall) + wide(low, tall) + [pltpu.VMEM((low, width), jnp.float32)],
        second_bond,
        *gathered[0],
        *gathered[1],
        *picked,
    )
    near_mid = call(
        functools.partial(rest_kernel, (0, 1)),
        "rest",
        [f32(tall, low)] * 2,
        2 * unit,
        [],
        ordered(second_bond, outer_first[0]),
        mid_high,
        mid_low,
    )
    regrouped = [near_mid[0], swap(near_mid[1], 1), swap(away_mid, 2)]
    grad = call(
        functools.partial(stem_kernel, groups),
        "grad_stem",
        [f32(2 * low, height)] * 2,
        3 * unit,
        [pltpu.VMEM((low, tall), jnp.float32)],
        first_high,
        first_low,
        turned_high,
        turned_low,
    )
    *grad, regrouped[0] = lax.optimization_barrier((*grad, regrouped[0]))
    outer = call(
        functools.partial(second_kernel, factor),
        "grad_second",
        [f32(2 * own, width)] * splits,
        3 * unit,
        [pltpu.VMEM((low, width), jnp.float32)],
        *regrouped,
        cotan_high,
        cotan_low,
        *outer_first,
    )
    sums = RingSum(outer)
    sums.step()
    grad = sums.after(*grad)
    sums.step()
    for _ in range(far - 3):
        sums.step()
    moved = sums.after(*pair_exchange(*grad))
    sums.step()
    placed = call(place_kernel, "place", [f32(height, width)], 2 * unit, [], first_bond, *moved)[0]
    return placed.reshape(1, height, width), sums.total[:own], sums.total[own:]


def solution(mesh):
    return jax.shard_map(
        on_device,
        mesh=mesh,
        in_specs=(
            P("gx", "gy", None),
            P("gx", "gy", None),
            P(("gx", "gy"), None),
            P(("gx", "gy"), None),
            P(),
            P(),
        ),
        out_specs=(P("gx", "gy", None), P(("gx", "gy"), None), P(("gx", "gy"), None)),
        check_vma=False,
    )
```
